512 devices in a mesh: row: 16 (over y, core), col: 32 (over x, z).
Axes of the slice: x: 4, y: 8, z: 8, core: 2. Of those that a mesh axis runs over, the one named last changes fastest.
Arguments:
- logits: float32 [65536, 256], P(('row', 'col')), may hold values from -6 to 6
- tile_values: bfloat16 [16, 32, 128, 128, 128], P('row', 'col'), may hold values from -0.0625 to 0.0625
- tile_rows: int32 [16, 32, 128], P('row', 'col'), may hold values from 0 to 31, as said below
- tile_cols: int32 [16, 32, 128], P('row', 'col'), may hold values from 0 to 15, as said below
- tile_counts: int32 [16, 32], P('row', 'col'), may hold values from 16 to 128, as said below
Outputs:
- propagated: float32 [65536, 256], P(('row', 'col'))
The draws below stay inside these ranges and needn't reach their ends.
Inputs may be any that keep to these rules, and one draw needn't show every extreme that they name: `tile_rows`: within a device's first tile_counts slots the pairs (row, column) are in ascending order, repeats possible, and block 32 - 1 of the row group meets block 16 - 1 of the column group on every device; later slots hold zeros. `tile_cols`: see tile_rows. `tile_counts`: each count is 128 divided by 1, 2, 4 or 8.
All inputs are finite; a program needn't handle non-finite values.
Results may differ from the reference program's by a relative error of at most 0.029.
Values may be sent and summed in bfloat16 or wider, within the bound.
A program may use at most 64 MiB of HBM per device.

```python
import jax
import jax.numpy as jnp
from jax import lax

TILE = 128
CLS = 256
CAP = 128
HOPS = 2
NODES = 65536
N_ROW = 16
N_COL = 32


def tile_layout(key):
    devices = N_ROW * N_COL
    key_shift, key_pick, key_other, key_row, key_col = jax.random.split(jax.random.fold_in(key, 11), 5)
    shifts = jax.random.randint(key_shift, (devices,), 0, 4)
    chosen = jax.random.randint(key_pick, (), 0, devices)
    second = (chosen + 1 + jax.random.randint(key_other, (), 0, devices - 1)) % devices
    device_index = jnp.arange(devices)
    shifts = jnp.where(device_index == chosen, 0, shifts)
    shifts = jnp.where(device_index == second, 3, shifts)
    totals = (CAP // jnp.left_shift(1, shifts)).astype(jnp.int32)
    row_pick = jax.random.randint(key_row, (devices, CAP), 0, N_COL)
    col_pick = jax.random.randint(key_col, (devices, CAP), 0, N_ROW)
    row_pick = row_pick.at[:, 0].set(N_COL - 1)
    col_pick = col_pick.at[:, 0].set(N_ROW - 1)
    slot_index = jnp.arange(CAP)[None, :]
    live = slot_index < totals[:, None]
    order_key = jnp.where(live, row_pick * N_ROW + col_pick, N_ROW * N_COL)
    sorted_keys = jnp.sort(order_key, axis=1)
    live_sorted = sorted_keys < N_ROW * N_COL
    rows = jnp.where(live_sorted, sorted_keys // N_ROW, 0).astype(jnp.int32)
    cols = jnp.where(live_sorted, sorted_keys % N_ROW, 0).astype(jnp.int32)
    return (rows.reshape(N_ROW, N_COL, CAP), cols.reshape(N_ROW, N_COL, CAP), totals.reshape(N_ROW, N_COL))


def draw_tile_rows(key, part):
    layout = tile_layout(key)
    return layout[0]


def draw_tile_cols(key, part):
    layout = tile_layout(key)
    return layout[1]


def draw_tile_counts(key, part):
    layout = tile_layout(key)
    return layout[2]


def block_levels(stream_key, extent, cuts, smallest, largest):
    level, own = 1.0, jax.random.fold_in(stream_key, 6)
    for dim, parts in cuts:
        heights = jnp.exp(jax.random.uniform(jax.random.fold_in(own, dim), (parts,), jnp.float32, smallest / len(cuts), largest / len(cuts)))
        level = level * jnp.repeat(heights, extent[dim] // parts).reshape([-1 if axis == dim else 1 for axis in range(len(extent))])
    return level


def centred(stream_key, dims, width, reach, cuts=(), held_as=jnp.bfloat16):
    array = width * jax.random.normal(stream_key, dims, jnp.float32)
    if cuts:
        array = array * block_levels(stream_key, dims, cuts, -0.22, 0.18)
    return jnp.clip(array, -reach, reach).astype(held_as)


def setup_inputs(seed: int = 0) -> dict:
    key_list = jax.random.split(jax.random.key(seed), 6)
    return {
        "logits": centred(key_list[0], (NODES, CLS), 1.0, 6.0, ((0, 512),), jnp.float32),
        "tile_values": centred(key_list[1], (N_ROW, N_COL, CAP, TILE, TILE), (CAP * 60) ** -0.5, 0.0625, ((0, 16), (1, 32))),
        "tile_rows": draw_tile_rows(jax.random.fold_in(key_list[5], 71), 0),
        "tile_cols": draw_tile_cols(jax.random.fold_in(key_list[5], 71), 0),
        "tile_counts": draw_tile_counts(jax.random.fold_in(key_list[5], 71), 0),
    }


def one_hop(current, logits, tile_values, tile_rows, tile_cols, tile_counts):
    panel = current.astype(jnp.bfloat16).reshape(N_ROW * N_COL, TILE, CLS)
    slot_index = jnp.arange(CAP, dtype=jnp.int32)

    def add_device(running, device):
        row_index = (device // N_COL).astype(jnp.int32)
        col_index = (device % N_COL).astype(jnp.int32)
        own_tiles = tile_values[row_index, col_index].astype(jnp.float32)
        target = tile_rows[row_index, col_index]
        source = tile_cols[row_index, col_index] * N_COL + col_index
        sources = panel[source].astype(jnp.float32)
        products = jnp.einsum("stk,skc->stc", own_tiles, sources, precision=lax.Precision.HIGHEST)
        live = slot_index < tile_counts[row_index, col_index]
        products = jnp.where(live[:, None, None], products, jnp.float32(0.0))
        partial_value = jnp.zeros((N_COL, TILE, CLS), jnp.float32).at[target].add(products)
        partial_value = partial_value.astype(jnp.bfloat16).astype(jnp.float32)
        return running.at[row_index].add(partial_value), None

    start = jnp.zeros((N_ROW, N_COL, TILE, CLS), jnp.float32)
    gathered, unused = lax.scan(add_device, start, jnp.arange(N_ROW * N_COL, dtype=jnp.int32))
    gathered = gathered.reshape(N_ROW * N_COL * TILE, CLS)
    return 0.9 * gathered + 0.1 * logits


def reference(logits, tile_values, tile_rows, tile_cols, tile_counts):
    current = logits
    for repeat in range(HOPS):
        current = one_hop(current, logits, tile_values, tile_rows, tile_cols, tile_counts)
    return current
```

```python
import functools

import jax
import jax.numpy as jnp
from jax import lax
from jax.experimental import pallas as pl
from jax.experimental.pallas import tpu as pltpu
from jax.sharding import PartitionSpec as P

HOPS = 2
HALVES = 2
LANES = 128
WINDOW = 3
UNROLL = 32
MESH = pl.DeviceIdType.MESH


def spread(k, n):
    m = (k + 1) // 2
    return n // 2 + m * (1 - 2 * lax.rem(k, 2)) if not isinstance(k, int) else n // 2 + (-m if k % 2 else m)


def kernel(nx, ny, nz, *refs):
    (tiles_hbm, rows_s, cols_s, counts_s, logits, out, tv, prod, last,
     panel00, panel01, panel10, panel11, part, xrecv, zsend, zrecv, zown,
     tile_sem, ag_send, ag_recv, sib_send, sib_recv, x_send, x_recv, z_send, z_recv) = refs
    panel = ((panel00, panel01), (panel10, panel11))
    cap, tile = tv.shape[0], tv.shape[1]
    nrow, ncol = 2 * ny, nx * nz
    row, col = lax.axis_index("row"), lax.axis_index("col")
    x, z = col // nz, lax.rem(col, nz)
    sibling = (row + 1 - 2 * lax.rem(row, 2), col)

    def at_y(d):
        return (lax.rem(row + 2 * d, nrow), col)

    def at_x(d):
        return (row, lax.rem(col + nz * d, ncol))

    def at_z(d):
        return (row, x * nz + lax.rem(z + d, nz))

    load = pltpu.make_async_copy(tiles_hbm.at[0, 0], tv, tile_sem)
    load.start()
    for h in range(HALVES):
        panel[0][h][row] = logits[:, h * LANES:(h + 1) * LANES].astype(jnp.bfloat16)

    barrier = pltpu.get_barrier_semaphore()
    peers = [at_y(d) for d in range(1, ny)] + [at_x(d) for d in range(1, nx)] + [at_z(d) for d in range(1, nz)] + [sibling]
    for peer in peers:
        pl.semaphore_signal(barrier, inc=1, device_id=peer, device_id_type=MESH)
    pl.semaphore_wait(barrier, len(peers))

    def remote(src, dst, send_sem, recv_sem, device):
        return pltpu.make_async_remote_copy(src_ref=src, dst_ref=dst, send_sem=send_sem, recv_sem=recv_sem,
                                            device_id=device, device_id_type=MESH)

    def gather_start(t, h):
        p = panel[t][h]

        def step(k, carry):
            remote(p.at[row], p.at[row], ag_send.at[t, h], ag_recv.at[t, h, k], at_y(spread(k, ny))).start()
            return carry

        lax.fori_loop(0, ny - 1, step, 0)
        remote(p.at[row], p.at[row], sib_send.at[t, h], sib_recv.at[t, h], sibling).start()

    def gather_finish(t, h):
        p = panel[t][h]

        def step(k, carry):
            source = lax.rem(row + nrow - 2 * spread(k, ny), nrow)
            block = p.at[source]
            remote(block, block, ag_send.at[t, h], ag_recv.at[t, h, k], sibling).wait_recv()
            remote(block, block, sib_send.at[t, h], sib_recv.at[t, h], sibling).start()
            return carry

        lax.fori_loop(0, ny - 1, step, 0)
        most = p.at[pl.ds(0, ny)]
        remote(most, most, sib_send.at[t, h], sib_recv.at[t, h], sibling).wait_recv()

    def products(t, h):
        p = panel[t][h]
        unroll = min(UNROLL, cap)

        def group(g, total):
            terms = [
                jnp.dot(tv[g * unroll + u], p[cols_s[0, 0, g * unroll + u]], preferred_element_type=jnp.float32)
                for u in range(unroll)
            ]
            for u in range(unroll):
                s = g * unroll + u
                same = (rows_s[0, 0, s] == rows_s[0, 0, jnp.maximum(s - 1, 0)]).astype(jnp.float32)
                total = total * same + terms[u]
                prod[s] = total.astype(jnp.bfloat16)
            return total

        lax.fori_loop(0, cap // unroll, group, jnp.zeros((tile, LANES), jnp.float32))

        def place(r, carry):
            part[t, h, r] = prod[last[r]]
            return carry

        lax.fori_loop(0, ncol, place, 0, unroll=4)

    def x_start(t, h, k):
        block = lax.rem(z + spread(k, nz), nz)
        for e in (2, 1, 3) if nx == 4 else range(1, nx):
            target = lax.rem(x + e, nx) * nz + block
            remote(part.at[t, h, target], xrecv.at[t, h, k, e - 1], x_send.at[t, h], x_recv.at[t, h, k], at_x(e)).start()

    def x_sum(t, h, k):
        arrived = xrecv.at[t, h, k]
        remote(arrived, arrived, x_send.at[t, h], x_recv.at[t, h, k], sibling).wait_recv()
        total = part[t, h, x * nz + lax.rem(z + spread(k, nz), nz)].astype(jnp.float32)
        for e in range(nx - 1):
            total += xrecv[t, h, k, e].astype(jnp.float32)
        return total

    def x_step(t, h, k):
        zsend[t, h, k] = x_sum(t, h, k).astype(jnp.bfloat16)
        remote(zsend.at[t, h, k], zrecv.at[t, h, k], z_send.at[t, h], z_recv.at[t, h], at_z(spread(k, nz))).start()

    def x_run(t, h, lo, hi, follow):
        def step(k, carry):
            x_step(t, h, k)
            if follow is not None:
                x_start(follow[0], follow[1], k + follow[2])
            return carry

        lax.fori_loop(lo, hi, step, 0)

    def x_last(t, h):
        zown[t, h] = x_sum(t, h, nz - 1)

    def finish(t, h):
        arrived = zrecv.at[t, h]
        remote(arrived, arrived, z_send.at[t, h], z_recv.at[t, h], sibling).wait_recv()
        total = zown[t, h]
        for k in range(nz - 1):
            total += zrecv[t, h, k].astype(jnp.float32)
        lanes = slice(h * LANES, (h + 1) * LANES)
        current = 0.9 * total + 0.1 * logits[:, lanes]
        if t + 1 < HOPS:
            panel[t + 1][h][row] = current.astype(jnp.bfloat16)
        else:
            out[:, lanes] = current

    def sent(t, h):
        some = panel[t][h].at[pl.ds(0, ny - 1)]
        remote(some, some, ag_send.at[t, h], ag_recv.at[t, h, 0], sibling).wait_send()
        some = panel[t][h].at[pl.ds(0, ny)]
        remote(some, some, sib_send.at[t, h], sib_recv.at[t, h], sibling).wait_send()
        some = part.at[t, h, pl.ds(0, (nx - 1) * nz)]
        remote(some, some, x_send.at[t, h], x_recv.at[t, h, 0], sibling).wait_send()
        some = zsend.at[t, h]
        remote(some, some, z_send.at[t, h], z_recv.at[t, h], sibling).wait_send()

    window = min(WINDOW, nz - 1)

    def x_open(t, h):
        for k in range(window):
            x_start(t, h, k)

    gather_start(0, 0)
    gather_start(0, 1)

    prod[cap] = jnp.zeros((tile, LANES), jnp.bfloat16)
    count = counts_s[0, 0]

    def find(r, carry):
        place = jnp.int32(0)
        step = cap
        while step:
            tried = place + step
            fits = (tried <= count) & (rows_s[0, 0, jnp.minimum(tried, cap) - 1] <= r)
            place = jnp.where(fits, tried, place)
            step //= 2
        found = (place > 0) & (rows_s[0, 0, jnp.maximum(place - 1, 0)] == r)
        last[r] = jnp.where(found, place - 1, cap)
        return carry

    lax.fori_loop(0, ncol, find, 0)
    load.wait()

    gather_finish(0, 0)
    products(0, 0)
    x_open(0, 0)
    gather_finish(0, 1)
    products(0, 1)
    x_run(0, 0, 0, nz - window, (0, 0, window))
    x_run(0, 0, nz - window, nz - 1, (0, 1, window - nz))
    x_last(0, 0)
    x_start(0, 1, window - 1)
    early = min(3, nz - window)
    x_run(0, 1, 0, early, (0, 1, window))
    finish(0, 0)
    gather_start(1, 0)
    x_run(0, 1, early, nz - window, (0, 1, window))
    x_run(0, 1, nz - window, nz - 1, None)
    x_last(0, 1)
    gather_finish(1, 0)
    products(1, 0)
    x_open(1, 0)
    finish(0, 1)
    gather_start(1, 1)
    x_run(1, 0, 0, nz - window, (1, 0, window))
    x_run(1, 0, nz - window, nz - 1, None)
    x_last(1, 0)
    gather_finish(1, 1)
    products(1, 1)
    x_open(1, 1)
    sent(0, 0)
    sent(0, 1)
    finish(1, 0)
    x_run(1, 1, 0, nz - window, (1, 1, window))
    x_run(1, 1, nz - window, nz - 1, None)
    x_last(1, 1)
    sent(1, 0)
    finish(1, 1)
    sent(1, 1)


def solution(mesh):
    nrow, ncol = mesh.shape["row"], mesh.shape["col"]
    ny = nrow // 2
    nx = 4 if ncol == 32 else 2
    nz = ncol // nx

    def body(logits, tile_values, tile_rows, tile_cols, tile_counts):
        cap, tile = tile_values.shape[2], tile_values.shape[3]
        half = jnp.bfloat16
        dma = pltpu.SemaphoreType.DMA
        both = (HOPS, HALVES)
        return pl.pallas_call(
            functools.partial(kernel, nx, ny, nz),
            out_shape=jax.ShapeDtypeStruct(logits.shape, jnp.float32),
            in_specs=[
                pl.BlockSpec(memory_space=pl.ANY),
                pl.BlockSpec(memory_space=pltpu.SMEM),
                pl.BlockSpec(memory_space=pltpu.SMEM),
                pl.BlockSpec(memory_space=pltpu.SMEM),
                pl.BlockSpec(memory_space=pltpu.VMEM),
            ],
            out_specs=pl.BlockSpec(memory_space=pltpu.VMEM),
            scratch_shapes=[
                pltpu.VMEM((cap, tile, tile), half),
                pltpu.VMEM((cap + 1, tile, LANES), half),
                pltpu.SMEM((ncol,), jnp.int32),
                *[pltpu.VMEM((nrow, tile, LANES), half) for unused in range(HOPS * HALVES)],
                pltpu.VMEM((*both, ncol, tile, LANES), half),
                pltpu.VMEM((*both, nz, nx - 1, tile, LANES), half),
                pltpu.VMEM((*both, nz - 1, tile, LANES), half),
                pltpu.VMEM((*both, nz - 1, tile, LANES), half),
                pltpu.VMEM((*both, tile, LANES), jnp.float32),
                dma,
                dma(both),
                dma((*both, ny - 1)),
                dma(both),
                dma(both),
                dma(both),
                dma((*both, nz)),
                dma(both),
                dma(both),
            ],
            compiler_params=pltpu.CompilerParams(
                collective_id=0, has_side_effects=True, vmem_limit_bytes=58 * 2**20
            ),
            name="propagate",
        )(tile_values, tile_rows, tile_cols, tile_counts, logits)

    return jax.shard_map(
        body,
        mesh=mesh,
        in_specs=(
            P(("row", "col"), None),
            P("row", "col", None, None, None),
            P("row", "col", None),
            P("row", "col", None),
            P("row", "col"),
        ),
        out_specs=P(("row", "col"), None),
        check_vma=False,
    )
```

```python
import functools

import jax
import jax.numpy as jnp
from jax import lax
from jax.experimental import pallas as pl
from jax.experimental.pallas import tpu as pltpu
from jax.sharding import PartitionSpec as P

HOPS = 2
HALVES = 2
LANES = 128
UNROLL = 64
ROWS = 80
MESH = pl.DeviceIdType.MESH


def spread(k, n):
    m = (k + 1) // 2
    return n // 2 + m * (1 - 2 * lax.rem(k, 2)) if not isinstance(k, int) else n // 2 + (-m if k % 2 else m)


def kernel(nx, ny, nz, *refs):
    (tiles_hbm, rows_hbm, cols_hbm, counts_s, logits_hbm, out, tv, prod, last, rows_s, cols_s, logits,
     panel00, panel01, panel10, panel11, part, xrecv, zsend, zrecv, zown, zfrecv, zfmid, xfsend, xfrecv,
     in_sems, ag_send, ag_recv, sib_send, sib_recv, x_send, x_recv, z_send, z_recv,
     zf_send, zf_recv, xf_send, xf_recv) = refs
    panel = ((panel00, panel01), (panel10, panel11))
    cap, tile = tv.shape[0], tv.shape[1]
    nrow, ncol = 2 * ny, nx * nz
    row, col = lax.axis_index("row"), lax.axis_index("col")
    x, z, core = col // nz, lax.rem(col, nz), lax.rem(row, 2)
    sibling = (row + 1 - 2 * core, col)
    turn = 1 - 2 * core
    upper, lower = pl.ds(0, ROWS), pl.ds(ROWS, tile - ROWS)

    def at_y(d):
        return (lax.rem(row + 2 * (d + ny), nrow), col)

    def at_x(d):
        return (row, lax.rem(col + nz * d, ncol))

    def at_z(d):
        return (row, x * nz + lax.rem(z + d + nz, nz))

    barrier = pltpu.get_barrier_semaphore()
    ways = (1, -1, 2, -2)
    peers = [at_y(d) for d in ways] + [at_x(d) for d in range(1, nx)] + [at_z(d) for d in range(1, nz)] + [sibling]
    for peer in peers:
        pl.semaphore_signal(barrier, inc=1, device_id=peer, device_id_type=MESH)
    loads = [
        pltpu.make_async_copy(logits_hbm, logits, in_sems.at[0]),
        pltpu.make_async_copy(rows_hbm, rows_s, in_sems.at[1]),
        pltpu.make_async_copy(cols_hbm, cols_s, in_sems.at[2]),
        pltpu.make_async_copy(tiles_hbm.at[0, 0], tv, in_sems.at[3]),
    ]
    for load in loads:
        load.start()
    loads[0].wait()
    for h in range(HALVES):
        panel[0][h][row] = logits[:, h * LANES:(h + 1) * LANES].astype(jnp.bfloat16)
    pl.semaphore_wait(barrier, len(peers))

    def remote(src, dst, send_sem, recv_sem, device):
        return pltpu.make_async_remote_copy(src_ref=src, dst_ref=dst, send_sem=send_sem, recv_sem=recv_sem,
                                            device_id=device, device_id_type=MESH)

    def gather_send(t, h, block, slot, d):
        p = panel[t][h]
        remote(p.at[block], p.at[block], ag_send.at[t, h], ag_recv.at[t, h, slot], at_y(d)).start()

    def gather_start(t, h):
        p = panel[t][h]
        for slot, d in enumerate((2, -2, 1, -1)):
            gather_send(t, h, row, slot, d)
        remote(p.at[row], p.at[row], sib_send.at[t, h], sib_recv.at[t, h], sibling).start()

    def gather_wait(t, h, slot, d):
        p = panel[t][h]
        source = lax.rem(row + nrow - 2 * d, nrow)
        block = p.at[source]
        remote(block, block, ag_send.at[t, h], ag_recv.at[t, h, slot], sibling).wait_recv()
        remote(block, block, sib_send.at[t, h], sib_recv.at[t, h], sibling).start()
        return source

    def gather_mid(t, h):
        first = []
        for slot, d in enumerate((2, -2)):
            p = panel[t][h]
            source = lax.rem(row + nrow - 2 * d, nrow)
            block = p.at[source]
            remote(block, block, ag_send.at[t, h], ag_recv.at[t, h, slot], sibling).wait_recv()
            gather_send(t, h, source, 4 + slot, d // 2)
            first.append(source)
        gather_send(t, h, lax.rem(row + nrow - 4 * turn, nrow), 6, 2 * turn)
        for source in first:
            block = panel[t][h].at[source]
            remote(block, block, sib_send.at[t, h], sib_recv.at[t, h], sibling).start()

    def gather_finish(t, h):
        for slot, d in ((2, 1), (3, -1), (4, 3), (5, -3), (6, 4)):
            gather_wait(t, h, slot, d)
        most = panel[t][h].at[pl.ds(0, ny)]
        remote(most, most, sib_send.at[t, h], sib_recv.at[t, h], sibling).wait_recv()

    def products(t, h):
        p = panel[t][h]
        unroll = min(UNROLL, cap)

        def group(g, total):
            terms = [
                jnp.dot(tv[g * unroll + u], p[cols_s[0, 0, g * unroll + u]], preferred_element_type=jnp.float32)
                for u in range(unroll)
            ]
            for u in range(unroll):
                s = g * unroll + u
                same = (rows_s[0, 0, s] == rows_s[0, 0, jnp.maximum(s - 1, 0)]).astype(jnp.float32)
                total = total * same + terms[u]
                prod[s] = total.astype(jnp.bfloat16)
            return total

        lax.fori_loop(0, cap // unroll, group, jnp.zeros((tile, LANES), jnp.float32))

        def place(r, carry):
            part[t, h, r // nz, lax.rem(r, nz)] = prod[last[r]]
            return carry

        lax.fori_loop(0, ncol, place, 0, unroll=4)

    def x_start(t, h, k):
        block = lax.rem(z + spread(k, nz), nz)
        for e in (2, 1, 3):
            target = lax.rem(x + e, nx)
            remote(part.at[t, h, target, block, upper], xrecv.at[t, h, k, e - 1], x_send.at[t, h], x_recv.at[t, h, k], at_x(e)).start()

    def x_sum(t, h, k):
        arrived = xrecv.at[t, h, k]
        remote(arrived, arrived, x_send.at[t, h], x_recv.at[t, h, k], sibling).wait_recv()
        total = part[t, h, x, lax.rem(z + spread(k, nz), nz), upper].astype(jnp.float32)
        for e in range(nx - 1):
            total += xrecv[t, h, k, e].astype(jnp.float32)
        return total

    def x_step(t, h, k):
        zsend[t, h, k] = x_sum(t, h, k).astype(jnp.bfloat16)
        remote(zsend.at[t, h, k], zrecv.at[t, h, k], z_send.at[t, h], z_recv.at[t, h], at_z(spread(k, nz))).start()

    def x_run(t, h, lo, hi):
        def step(k, carry):
            x_step(t, h, k)
            return carry

        lax.fori_loop(lo, hi, step, 0)

    def x_last(t, h):
        zown[t, h] = x_sum(t, h, nz - 1)

    def zf_block(t, h, d):
        return part.at[t, h, :, lax.rem(z + d + nz, nz), lower]

    def zf_send_to(t, h, source, slot, sem, d):
        remote(source, zfrecv.at[t, h, slot], zf_send.at[t, h], zf_recv.at[t, h, sem], at_z(d)).start()

    def zf_start(t, h):
        zf_send_to(t, h, zf_block(t, h, 4 * turn), 0, 0, 2 * turn)
        zf_send_to(t, h, zf_block(t, h, 3 * turn), 1, 0, turn)
        zf_send_to(t, h, zf_block(t, h, -3 * turn), 2, 1, -turn)
        zf_send_to(t, h, zf_block(t, h, turn), 3, 2, turn)
        zf_send_to(t, h, zf_block(t, h, -turn), 4, 2, -turn)

    def zf_wait(t, h, lo, n, sem):
        arrived = zfrecv.at[t, h, pl.ds(lo, n)]
        remote(arrived, arrived, zf_send.at[t, h], zf_recv.at[t, h, sem], sibling).wait_recv()

    def zf_own(t, h, d):
        return part[t, h, :, lax.rem(z + d + nz, nz), lower].astype(jnp.float32)

    def zf_mid(t, h):
        zf_wait(t, h, 0, 2, 0)
        total = zf_own(t, h, 2 * turn) + zfrecv[t, h, 0].astype(jnp.float32) + zfrecv[t, h, 1].astype(jnp.float32)
        zfmid[t, h, 0] = total.astype(jnp.bfloat16)
        zf_send_to(t, h, zfmid.at[t, h, 0], 5, 2, 2 * turn)
        zf_wait(t, h, 2, 1, 1)
        total = zf_own(t, h, -2 * turn) + zfrecv[t, h, 2].astype(jnp.float32)
        zfmid[t, h, 1] = total.astype(jnp.bfloat16)
        zf_send_to(t, h, zfmid.at[t, h, 1], 6, 2, -2 * turn)

    def zf_end(t, h):
        zf_wait(t, h, 3, 4, 2)
        total = zf_own(t, h, 0)
        for slot in range(3, 7):
            total += zfrecv[t, h, slot].astype(jnp.float32)
        xfsend[t, h] = total.astype(jnp.bfloat16)
        for e in (2, 1, 3):
            remote(xfsend.at[t, h, lax.rem(x + e, nx)], xfrecv.at[t, h, e - 1], xf_send.at[t, h], xf_recv.at[t, h], at_x(e)).start()

    def finish(t, h):
        arrived = zrecv.at[t, h]
        remote(arrived, arrived, z_send.at[t, h], z_recv.at[t, h], sibling).wait_recv()
        total = zown[t, h]
        for k in range(nz - 1):
            total += zrecv[t, h, k].astype(jnp.float32)
        lanes = slice(h * LANES, (h + 1) * LANES)

        def store(part_rows, total):
            current = 0.9 * total + 0.1 * logits[part_rows, lanes]
            if t + 1 < HOPS:
                panel[t + 1][h][row, part_rows] = current.astype(jnp.bfloat16)
            else:
                out[part_rows, lanes] = current

        store(slice(0, ROWS), total)
        arrived = xfrecv.at[t, h]
        remote(arrived, arrived, xf_send.at[t, h], xf_recv.at[t, h], sibling).wait_recv()
        total = xfsend[t, h, x].astype(jnp.float32)
        for e in range(nx - 1):
            total += xfrecv[t, h, e].astype(jnp.float32)
        store(slice(ROWS, tile), total)

    def sent(t, h):
        some = panel[t][h].at[pl.ds(0, ny - 1)]
        remote(some, some, ag_send.at[t, h], ag_recv.at[t, h, 0], sibling).wait_send()
        some = panel[t][h].at[pl.ds(0, ny)]
        remote(some, some, sib_send.at[t, h], sib_recv.at[t, h], sibling).wait_send()
        some = xrecv.at[t, h]
        remote(some, some, x_send.at[t, h], x_recv.at[t, h, 0], sibling).wait_send()
        some = zsend.at[t, h]
        remote(some, some, z_send.at[t, h], z_recv.at[t, h], sibling).wait_send()
        some = zfrecv.at[t, h]
        remote(some, some, zf_send.at[t, h], zf_recv.at[t, h, 0], sibling).wait_send()
        some = xfrecv.at[t, h]
        remote(some, some, xf_send.at[t, h], xf_recv.at[t, h], sibling).wait_send()

    def open_all(t, h):
        def step(k, carry):
            x_start(t, h, k)
            return carry

        zf_start(t, h)
        lax.fori_loop(0, nz, step, 0)

    gather_start(0, 0)

    prod[cap] = jnp.zeros((tile, LANES), jnp.bfloat16)
    count = counts_s[0, 0]

    def find(r, carry):
        place = jnp.int32(0)
        step = cap
        while step:
            tried = place + step
            fits = (tried <= count) & (rows_s[0, 0, jnp.minimum(tried, cap) - 1] <= r)
            place = jnp.where(fits, tried, place)
            step //= 2
        found = (place > 0) & (rows_s[0, 0, jnp.maximum(place - 1, 0)] == r)
        last[r] = jnp.where(found, place - 1, cap)
        return carry

    loads[1].wait()
    loads[2].wait()
    lax.fori_loop(0, ncol // 2, find, 0)
    gather_mid(0, 0)
    gather_start(0, 1)
    lax.fori_loop(ncol // 2, ncol, find, 0)
    loads[3].wait()

    gather_finish(0, 0)
    products(0, 0)
    open_all(0, 0)
    gather_mid(0, 1)
    x_run(0, 0, 0, 2)
    zf_mid(0, 0)
    gather_finish(0, 1)
    products(0, 1)
    open_all(0, 1)
    x_run(0, 0, 2, nz - 1)
    x_last(0, 0)
    zf_end(0, 0)
    x_run(0, 1, 0, 2)
    zf_mid(0, 1)
    finish(0, 0)
    gather_start(1, 0)
    x_run(0, 1, 2, nz - 1)
    x_last(0, 1)
    zf_end(0, 1)
    gather_mid(1, 0)
    finish(0, 1)
    gather_start(1, 1)
    gather_finish(1, 0)
    products(1, 0)
    open_all(1, 0)
    gather_mid(1, 1)
    x_run(1, 0, 0, 2)
    zf_mid(1, 0)
    gather_finish(1, 1)
    products(1, 1)
    open_all(1, 1)
    sent(0, 0)
    sent(0, 1)
    x_run(1, 0, 2, nz - 1)
    x_last(1, 0)
    zf_end(1, 0)
    x_run(1, 1, 0, 2)
    zf_mid(1, 1)
    finish(1, 0)
    x_run(1, 1, 2, nz - 1)
    x_last(1, 1)
    zf_end(1, 1)
    sent(1, 0)
    finish(1, 1)
    sent(1, 1)


def solution(mesh):
    nrow, ncol = mesh.shape["row"], mesh.shape["col"]
    ny = nrow // 2
    nx = 4 if ncol == 32 else 2
    nz = ncol // nx

    def body(logits, tile_values, tile_rows, tile_cols, tile_counts):
        cap, tile = tile_values.shape[2], tile_values.shape[3]
        half = jnp.bfloat16
        dma = pltpu.SemaphoreType.DMA
        both = (HOPS, HALVES)
        return pl.pallas_call(
            functools.partial(kernel, nx, ny, nz),
            out_shape=jax.ShapeDtypeStruct(logits.shape, jnp.float32),
            in_specs=[
                pl.BlockSpec(memory_space=pl.ANY),
                pl.BlockSpec(memory_space=pl.ANY),
                pl.BlockSpec(memory_space=pl.ANY),
                pl.BlockSpec(memory_space=pltpu.SMEM),
                pl.BlockSpec(memory_space=pl.ANY),
            ],
            out_specs=pl.BlockSpec(memory_space=pltpu.VMEM),
            scratch_shapes=[
                pltpu.VMEM((cap, tile, tile), half),
                pltpu.VMEM((cap + 1, tile, LANES), half),
                pltpu.SMEM((ncol,), jnp.int32),
                pltpu.SMEM((1, 1, cap), jnp.int32),
                pltpu.SMEM((1, 1, cap), jnp.int32),
                pltpu.VMEM(logits.shape, jnp.float32),
                *[pltpu.VMEM((nrow, tile, LANES), half) for unused in range(HOPS * HALVES)],
                pltpu.VMEM((*both, nx, nz, tile, LANES), half),
                pltpu.VMEM((*both, nz, nx - 1, ROWS, LANES), half),
                pltpu.VMEM((*both, nz - 1, ROWS, LANES), half),
                pltpu.VMEM((*both, nz - 1, ROWS, LANES), half),
                pltpu.VMEM((*both, ROWS, LANES), jnp.float32),
                pltpu.VMEM((*both, 7, nx, tile - ROWS, LANES), half),
                pltpu.VMEM((*both, 2, nx, tile - ROWS, LANES), half),
                pltpu.VMEM((*both, nx, tile - ROWS, LANES), half),
                pltpu.VMEM((*both, nx - 1, tile - ROWS, LANES), half),
                dma((4,)),
                dma(both),
                dma((*both, 7)),
                dma(both),
                dma(both),
                dma(both),
                dma((*both, nz)),
                dma(both),
                dma(both),
                dma(both),
                dma((*both, 3)),
                dma(both),
                dma(both),
            ],
            compiler_params=pltpu.CompilerParams(
                collective_id=0, has_side_effects=True, vmem_limit_bytes=58 * 2**20
            ),
            name="propagate",
        )(tile_values, tile_rows, tile_cols, tile_counts, logits)

    return jax.shard_map(
        body,
        mesh=mesh,
        in_specs=(
            P(("row", "col"), None),
            P("row", "col", None, None, None),
            P("row", "col", None),
            P("row", "col", None),
            P("row", "col"),
        ),
        out_specs=P(("row", "col"), None),
        check_vma=False,
    )
```

```python
import functools

import jax
import jax.numpy as jnp
from jax import lax
from jax.experimental import pallas as pl
from jax.experimental.pallas import tpu as pltpu
from jax.sharding import PartitionSpec as P

HOPS = 2
HALVES = 2
LANES = 128
UNROLL = 64
ROWS = 80
BOUNDS = (0, 2, 4, 6, 8)
MESH = pl.DeviceIdType.MESH


def spread(k, n):
    m = (k + 1) // 2
    return n // 2 + m * (1 - 2 * lax.rem(k, 2)) if not isinstance(k, int) else n // 2 + (-m if k % 2 else m)


def kernel(nx, ny, nz, *refs):
    (tiles_hbm, rows_hbm, cols_hbm, counts_s, logits_hbm, out, tv, prod, last, rows_s, cols_s, logits,
     panel00, panel01, panel10, panel11, part, xrecv, zsend, zrecv, zown, zfrecv, zfmid, xfsend, xfrecv,
     in_sems, ag_send, ag_recv, sib_send, sib_recv, x_send, x_recv, z_send, z_recv,
     zf_send, zf_recv, xf_send, xf_recv) = refs
    panel = ((panel00, panel01), (panel10, panel11))
    cap, tile = tv.shape[0], tv.shape[1]
    nrow, ncol = 2 * ny, nx * nz
    row, col = lax.axis_index("row"), lax.axis_index("col")
    x, z, core = col // nz, lax.rem(col, nz), lax.rem(row, 2)
    sibling = (row + 1 - 2 * core, col)
    turn = 1 - 2 * core
    upper, lower = pl.ds(0, ROWS), pl.ds(ROWS, tile - ROWS)

    def at_y(d):
        return (lax.rem(row + 2 * (d + ny), nrow), col)

    def at_x(d):
        return (row, lax.rem(col + nz * d, ncol))

    def at_z(d):
        return (row, x * nz + lax.rem(z + d + nz, nz))

    barrier = pltpu.get_barrier_semaphore()
    ways = (1, -1, 2, -2)
    peers = [at_y(d) for d in ways] + [at_x(d) for d in range(1, nx)] + [at_z(d) for d in range(1, nz)] + [sibling]
    for peer in peers:
        pl.semaphore_signal(barrier, inc=1, device_id=peer, device_id_type=MESH)
    loads = [
        pltpu.make_async_copy(logits_hbm, logits, in_sems.at[0]),
        pltpu.make_async_copy(rows_hbm, rows_s, in_sems.at[1]),
        pltpu.make_async_copy(cols_hbm, cols_s, in_sems.at[2]),
        pltpu.make_async_copy(tiles_hbm.at[0, 0], tv, in_sems.at[3]),
    ]
    for load in loads:
        load.start()
    loads[0].wait()
    for h in range(HALVES):
        panel[0][h][row] = logits[:, h * LANES:(h + 1) * LANES].astype(jnp.bfloat16)
    pl.semaphore_wait(barrier, len(peers))

    def remote(src, dst, send_sem, recv_sem, device):
        return pltpu.make_async_remote_copy(src_ref=src, dst_ref=dst, send_sem=send_sem, recv_sem=recv_sem,
                                            device_id=device, device_id_type=MESH)

    def gather_send(t, h, block, slot, d):
        p = panel[t][h]
        remote(p.at[block], p.at[block], ag_send.at[t, h], ag_recv.at[t, h, slot], at_y(d)).start()

    def gather_start(t, h):
        p = panel[t][h]
        for slot, d in enumerate((2, -2, 1, -1)):
            gather_send(t, h, row, slot, d)
        remote(p.at[row], p.at[row], sib_send.at[t, h], sib_recv.at[t, h], sibling).start()

    def gather_wait(t, h, slot, d):
        p = panel[t][h]
        source = lax.rem(row + nrow - 2 * d, nrow)
        block = p.at[source]
        remote(block, block, ag_send.at[t, h], ag_recv.at[t, h, slot], sibling).wait_recv()
        remote(block, block, sib_send.at[t, h], sib_recv.at[t, h], sibling).start()
        return source

    def gather_mid(t, h):
        first = []
        for slot, d in enumerate((2, -2)):
            p = panel[t][h]
            source = lax.rem(row + nrow - 2 * d, nrow)
            block = p.at[source]
            remote(block, block, ag_send.at[t, h], ag_recv.at[t, h, slot], sibling).wait_recv()
            gather_send(t, h, source, 4 + slot, d // 2)
            first.append(source)
        gather_send(t, h, lax.rem(row + nrow - 4 * turn, nrow), 6, 2 * turn)
        for source in first:
            block = panel[t][h].at[source]
            remote(block, block, sib_send.at[t, h], sib_recv.at[t, h], sibling).start()

    def gather_finish(t, h):
        for slot, d in ((2, 1), (3, -1), (4, 3), (5, -3), (6, 4)):
            gather_wait(t, h, slot, d)
        most = panel[t][h].at[pl.ds(0, ny)]
        remote(most, most, sib_send.at[t, h], sib_recv.at[t, h], sibling).wait_recv()

    def products(t, h):
        p = panel[t][h]
        unroll = min(UNROLL, cap)

        def group(g, total):
            terms = [
                jnp.dot(tv[g * unroll + u], p[cols_s[0, 0, g * unroll + u]], preferred_element_type=jnp.float32)
                for u in range(unroll)
            ]
            for u in range(unroll):
                s = g * unroll + u
                same = (rows_s[0, 0, s] == rows_s[0, 0, jnp.maximum(s - 1, 0)]).astype(jnp.float32)
                total = total * same + terms[u]
                prod[s] = total.astype(jnp.bfloat16)
            return total

        lax.fori_loop(0, cap // unroll, group, jnp.zeros((tile, LANES), jnp.float32))

        def place(k, carry):
            block = lax.rem(z + spread(k, nz), nz)
            for target in range(nx):
                part[t, h, target, k] = prod[last[target * nz + block]]
            return carry

        lax.fori_loop(0, nz, place, 0)

    def x_start(t, h, g):
        some = pl.ds(BOUNDS[g], BOUNDS[g + 1] - BOUNDS[g])
        for e in (2, 1, 3):
            target = lax.rem(x + e, nx)
            remote(part.at[t, h, target, some, upper], xrecv.at[t, h, e - 1, some], x_send.at[t, h], x_recv.at[t, h, g], at_x(e)).start()

    def x_sum(t, h, k):
        total = part[t, h, x, k, upper].astype(jnp.float32)
        for e in range(nx - 1):
            total += xrecv[t, h, e, k].astype(jnp.float32)
        return total

    def x_run(t, h, first, past):
        for g in range(first, past):
            lo, hi = BOUNDS[g], BOUNDS[g + 1]
            arrived = xrecv.at[t, h, :, pl.ds(lo, hi - lo)]
            remote(arrived, arrived, x_send.at[t, h], x_recv.at[t, h, g], sibling).wait_recv()

            def step(k, carry):
                zsend[t, h, k] = x_sum(t, h, k).astype(jnp.bfloat16)
                remote(zsend.at[t, h, k], zrecv.at[t, h, k], z_send.at[t, h], z_recv.at[t, h], at_z(spread(k, nz))).start()
                return carry

            lax.fori_loop(lo, min(hi, nz - 1), step, 0)
        if past == len(BOUNDS) - 1:
            zown[t, h] = x_sum(t, h, nz - 1)

    def zf_block(t, h, k):
        return part.at[t, h, :, k, lower]

    def zf_send_to(t, h, source, slot, sem, d):
        remote(source, zfrecv.at[t, h, slot], zf_send.at[t, h], zf_recv.at[t, h, sem], at_z(d)).start()

    def zf_start(t, h):
        zf_send_to(t, h, zf_block(t, h, 0), 0, 0, 2 * turn)
        zf_send_to(t, h, zf_block(t, h, 1 + core), 1, 0, turn)
        zf_send_to(t, h, zf_block(t, h, 2 - core), 2, 1, -turn)
        zf_send_to(t, h, zf_block(t, h, 5 + core), 3, 2, turn)
        zf_send_to(t, h, zf_block(t, h, 6 - core), 4, 2, -turn)

    def zf_wait(t, h, lo, n, sem):
        arrived = zfrecv.at[t, h, pl.ds(lo, n)]
        remote(arrived, arrived, zf_send.at[t, h], zf_recv.at[t, h, sem], sibling).wait_recv()

    def zf_own(t, h, k):
        return part[t, h, :, k, lower].astype(jnp.float32)

    def zf_mid(t, h):
        zf_wait(t, h, 0, 2, 0)
        total = zf_own(t, h, 3 + core) + zfrecv[t, h, 0].astype(jnp.float32) + zfrecv[t, h, 1].astype(jnp.float32)
        zfmid[t, h, 0] = total.astype(jnp.bfloat16)
        zf_send_to(t, h, zfmid.at[t, h, 0], 5, 2, 2 * turn)
        zf_wait(t, h, 2, 1, 1)
        total = zf_own(t, h, 4 - core) + zfrecv[t, h, 2].astype(jnp.float32)
        zfmid[t, h, 1] = total.astype(jnp.bfloat16)
        zf_send_to(t, h, zfmid.at[t, h, 1], 6, 2, -2 * turn)

    def zf_end(t, h):
        zf_wait(t, h, 3, 4, 2)
        total = zf_own(t, h, nz - 1)
        for slot in range(3, 7):
            total += zfrecv[t, h, slot].astype(jnp.float32)
        xfsend[t, h] = total.astype(jnp.bfloat16)
        for e in (2, 1, 3):
            remote(xfsend.at[t, h, lax.rem(x + e, nx)], xfrecv.at[t, h, e - 1], xf_send.at[t, h], xf_recv.at[t, h], at_x(e)).start()

    def finish(t, h):
        arrived = zrecv.at[t, h]
        remote(arrived, arrived, z_send.at[t, h], z_recv.at[t, h], sibling).wait_recv()
        total = zown[t, h]
        for k in range(nz - 1):
            total += zrecv[t, h, k].astype(jnp.float32)
        lanes = slice(h * LANES, (h + 1) * LANES)

        def store(part_rows, total):
            current = 0.9 * total + 0.1 * logits[part_rows, lanes]
            if t + 1 < HOPS:
                panel[t + 1][h][row, part_rows] = current.astype(jnp.bfloat16)
            else:
                out[part_rows, lanes] = current

        store(slice(0, ROWS), total)
        arrived = xfrecv.at[t, h]
        remote(arrived, arrived, xf_send.at[t, h], xf_recv.at[t, h], sibling).wait_recv()
        total = xfsend[t, h, x].astype(jnp.float32)
        for e in range(nx - 1):
            total += xfrecv[t, h, e].astype(jnp.float32)
        store(slice(ROWS, tile), total)

    def sent(t, h):
        some = panel[t][h].at[pl.ds(0, ny - 1)]
        remote(some, some, ag_send.at[t, h], ag_recv.at[t, h, 0], sibling).wait_send()
        some = panel[t][h].at[pl.ds(0, ny)]
        remote(some, some, sib_send.at[t, h], sib_recv.at[t, h], sibling).wait_send()
        some = xrecv.at[t, h]
        remote(some, some, x_send.at[t, h], x_recv.at[t, h, 0], sibling).wait_send()
        some = zsend.at[t, h]
        remote(some, some, z_send.at[t, h], z_recv.at[t, h], sibling).wait_send()
        some = zfrecv.at[t, h]
        remote(some, some, zf_send.at[t, h], zf_recv.at[t, h, 0], sibling).wait_send()
        some = xfrecv.at[t, h]
        remote(some, some, xf_send.at[t, h], xf_recv.at[t, h], sibling).wait_send()

    groups = len(BOUNDS) - 1

    def open_all(t, h):
        zf_start(t, h)
        for g in range(groups):
            x_start(t, h, g)

    gather_start(0, 0)

    prod[cap] = jnp.zeros((tile, LANES), jnp.bfloat16)
    count = counts_s[0, 0]

    def find(r, carry):
        place = jnp.int32(0)
        step = cap
        while step:
            tried = place + step
            fits = (tried <= count) & (rows_s[0, 0, jnp.minimum(tried, cap) - 1] <= r)
            place = jnp.where(fits, tried, place)
            step //= 2
        found = (place > 0) & (rows_s[0, 0, jnp.maximum(place - 1, 0)] == r)
        last[r] = jnp.where(found, place - 1, cap)
        return carry

    loads[1].wait()
    loads[2].wait()
    lax.fori_loop(0, ncol // 2, find, 0)
    gather_mid(0, 0)
    gather_start(0, 1)
    lax.fori_loop(ncol // 2, ncol, find, 0)
    loads[3].wait()

    gather_finish(0, 0)
    products(0, 0)
    open_all(0, 0)
    gather_mid(0, 1)
    x_run(0, 0, 0, 1)
    zf_mid(0, 0)
    gather_finish(0, 1)
    products(0, 1)
    open_all(0, 1)
    x_run(0, 0, 1, groups)
    zf_end(0, 0)
    x_run(0, 1, 0, 1)
    zf_mid(0, 1)
    finish(0, 0)
    gather_start(1, 0)
    x_run(0, 1, 1, groups)
    zf_end(0, 1)
    gather_mid(1, 0)
    finish(0, 1)
    gather_start(1, 1)
    gather_finish(1, 0)
    products(1, 0)
    open_all(1, 0)
    gather_mid(1, 1)
    x_run(1, 0, 0, 1)
    zf_mid(1, 0)
    gather_finish(1, 1)
    products(1, 1)
    open_all(1, 1)
    sent(0, 0)
    sent(0, 1)
    x_run(1, 0, 1, groups)
    zf_end(1, 0)
    x_run(1, 1, 0, 1)
    zf_mid(1, 1)
    finish(1, 0)
    x_run(1, 1, 1, groups)
    zf_end(1, 1)
    sent(1, 0)
    finish(1, 1)
    sent(1, 1)


def solution(mesh):
    nrow, ncol = mesh.shape["row"], mesh.shape["col"]
    ny = nrow // 2
    nx = 4 if ncol == 32 else 2
    nz = ncol // nx

    def body(logits, tile_values, tile_rows, tile_cols, tile_counts):
        cap, tile = tile_values.shape[2], tile_values.shape[3]
        half = jnp.bfloat16
        dma = pltpu.SemaphoreType.DMA
        both = (HOPS, HALVES)
        return pl.pallas_call(
            functools.partial(kernel, nx, ny, nz),
            out_shape=jax.ShapeDtypeStruct(logits.shape, jnp.float32),
            in_specs=[
                pl.BlockSpec(memory_space=pl.ANY),
                pl.BlockSpec(memory_space=pl.ANY),
                pl.BlockSpec(memory_space=pl.ANY),
                pl.BlockSpec(memory_space=pltpu.SMEM),
                pl.BlockSpec(memory_space=pl.ANY),
            ],
            out_specs=pl.BlockSpec(memory_space=pltpu.VMEM),
            scratch_shapes=[
                pltpu.VMEM((cap, tile, tile), half),
                pltpu.VMEM((cap + 1, tile, LANES), half),
                pltpu.SMEM((ncol,), jnp.int32),
                pltpu.SMEM((1, 1, cap), jnp.int32),
                pltpu.SMEM((1, 1, cap), jnp.int32),
                pltpu.VMEM(logits.shape, jnp.float32),
                *[pltpu.VMEM((nrow, tile, LANES), half) for unused in range(HOPS * HALVES)],
                pltpu.VMEM((*both, nx, nz, tile, LANES), half),
                pltpu.VMEM((*both, nx - 1, nz, ROWS, LANES), half),
                pltpu.VMEM((*both, nz - 1, ROWS, LANES), half),
                pltpu.VMEM((*both, nz - 1, ROWS, LANES), half),
                pltpu.VMEM((*both, ROWS, LANES), jnp.float32),
                pltpu.VMEM((*both, 7, nx, tile - ROWS, LANES), half),
                pltpu.VMEM((*both, 2, nx, tile - ROWS, LANES), half),
                pltpu.VMEM((*both, nx, tile - ROWS, LANES), half),
                pltpu.VMEM((*both, nx - 1, tile - ROWS, LANES), half),
                dma((4,)),
                dma(both),
                dma((*both, 7)),
                dma(both),
                dma(both),
                dma(both),
                dma((*both, nz)),
                dma(both),
                dma(both),
                dma(both),
                dma((*both, 3)),
                dma(both),
                dma(both),
            ],
            compiler_params=pltpu.CompilerParams(
                collective_id=0, has_side_effects=True, vmem_limit_bytes=58 * 2**20
            ),
            name="propagate",
        )(tile_values, tile_rows, tile_cols, tile_counts, logits)

    return jax.shard_map(
        body,
        mesh=mesh,
        in_specs=(
            P(("row", "col"), None),
            P("row", "col", None, None, None),
            P("row", "col", None),
            P("row", "col", None),
            P("row", "col"),
        ),
        out_specs=P(("row", "col"), None),
        check_vma=False,
    )
```

```python
import functools

import jax
import jax.numpy as jnp
from jax import lax
from jax.experimental import pallas as pl
from jax.experimental.pallas import tpu as pltpu
from jax.sharding import PartitionSpec as P

HOPS = 2
HALVES = 2
LANES = 128
UNROLL = 128
ROWS = 80
BOUNDS = (0, 3, 6, 8)
OFFSETS = (4, 3, -3, 1, -1, 0, 2, -2)
STEPS = (2, 1, -1, 1, -1, 0, 2, -2)
OWN = 5
MESH = pl.DeviceIdType.MESH


def kernel(nx, ny, nz, *refs):
    (tiles_hbm, rows_hbm, cols_hbm, counts_s, logits_hbm, out, tv, prod, last, rows_s, cols_s, logits,
     panel00, panel01, panel10, panel11, part, xrecv, zsend, zrecv, zown, zfrecv, zfmid, xfsend, xfrecv,
     in_sems, ag_send, ag_recv, sib_send, sib_recv, x_send, x_recv, z_send, z_recv,
     zf_send, zf_recv, xf_send, xf_recv) = refs
    panel = ((panel00, panel01), (panel10, panel11))
    cap, tile = tv.shape[0], tv.shape[1]
    nrow, ncol = 2 * ny, nx * nz
    row, col = lax.axis_index("row"), lax.axis_index("col")
    x, z, core = col // nz, lax.rem(col, nz), lax.rem(row, 2)
    sibling = (row + 1 - 2 * core, col)
    turn = 1 - 2 * core
    upper, lower = pl.ds(0, ROWS), pl.ds(ROWS, tile - ROWS)

    def at_y(d):
        return (lax.rem(row + 2 * (d + ny), nrow), col)

    def at_x(d):
        return (row, lax.rem(col + nz * d, ncol))

    def at_z(d):
        return (row, x * nz + lax.rem(z + d + nz, nz))

    barrier = pltpu.get_barrier_semaphore()
    ways = (1, -1, 2, -2)
    peers = [at_y(d) for d in ways] + [at_x(d) for d in range(1, nx)] + [at_z(d) for d in ways] + [sibling]
    for peer in peers:
        pl.semaphore_signal(barrier, inc=1, device_id=peer, device_id_type=MESH)
    loads = [
        pltpu.make_async_copy(logits_hbm, logits, in_sems.at[0]),
        pltpu.make_async_copy(rows_hbm, rows_s, in_sems.at[1]),
        pltpu.make_async_copy(cols_hbm, cols_s, in_sems.at[2]),
        pltpu.make_async_copy(tiles_hbm.at[0, 0], tv, in_sems.at[3]),
    ]
    for load in loads:
        load.start()
    loads[0].wait()
    for h in range(HALVES):
        panel[0][h][row] = logits[:, h * LANES:(h + 1) * LANES].astype(jnp.bfloat16)
    pl.semaphore_wait(barrier, len(peers))

    def remote(src, dst, send_sem, recv_sem, device):
        return pltpu.make_async_remote_copy(src_ref=src, dst_ref=dst, send_sem=send_sem, recv_sem=recv_sem,
                                            device_id=device, device_id_type=MESH)

    def gather_send(t, h, block, slot, d):
        p = panel[t][h]
        remote(p.at[block], p.at[block], ag_send.at[t, h], ag_recv.at[t, h, slot], at_y(d)).start()

    def gather_start(t, h):
        p = panel[t][h]
        for slot, d in enumerate((2, -2, 1, -1)):
            gather_send(t, h, row, slot, d)
        remote(p.at[row], p.at[row], sib_send.at[t, h], sib_recv.at[t, h], sibling).start()

    def gather_wait(t, h, slot, d):
        p = panel[t][h]
        source = lax.rem(row + nrow - 2 * d, nrow)
        block = p.at[source]
        remote(block, block, ag_send.at[t, h], ag_recv.at[t, h, slot], sibling).wait_recv()
        remote(block, block, sib_send.at[t, h], sib_recv.at[t, h], sibling).start()
        return source

    def gather_mid(t, h):
        first = []
        for slot, d in enumerate((2, -2)):
            p = panel[t][h]
            source = lax.rem(row + nrow - 2 * d, nrow)
            block = p.at[source]
            remote(block, block, ag_send.at[t, h], ag_recv.at[t, h, slot], sibling).wait_recv()
            gather_send(t, h, source, 4 + slot, d // 2)
            first.append(source)
        gather_send(t, h, lax.rem(row + nrow - 4 * turn, nrow), 6, 2 * turn)
        for source in first:
            block = panel[t][h].at[source]
            remote(block, block, sib_send.at[t, h], sib_recv.at[t, h], sibling).start()

    def gather_finish(t, h):
        for slot, d in ((2, 1), (3, -1), (4, 3), (5, -3), (6, 4)):
            gather_wait(t, h, slot, d)
        most = panel[t][h].at[pl.ds(0, ny)]
        remote(most, most, sib_send.at[t, h], sib_recv.at[t, h], sibling).wait_recv()

    def products(t, h):
        p = panel[t][h]
        unroll = min(UNROLL, cap)

        def group(g, total):
            terms = [
                jnp.dot(tv[g * unroll + u], p[cols_s[0, 0, g * unroll + u]], preferred_element_type=jnp.float32)
                for u in range(unroll)
            ]
            for u in range(unroll):
                s = g * unroll + u
                same = (rows_s[0, 0, s] == rows_s[0, 0, jnp.maximum(s - 1, 0)]).astype(jnp.float32)
                total = total * same + terms[u]
                prod[s] = total.astype(jnp.bfloat16)
            return total

        lax.fori_loop(0, cap // unroll, group, jnp.zeros((tile, LANES), jnp.float32))

        for k, d in enumerate(OFFSETS):
            block = lax.rem(z + d * turn + nz, nz)
            for target in range(nx):
                part[t, h, target, k] = prod[last[target * nz + block]]

    def x_start(t, h, g):
        some = pl.ds(BOUNDS[g], BOUNDS[g + 1] - BOUNDS[g])
        for e in (2, 1, 3):
            target = lax.rem(x + e, nx)
            remote(part.at[t, h, target, some, upper], xrecv.at[t, h, e - 1, some], x_send.at[t, h], x_recv.at[t, h, g], at_x(e)).start()

    def x_sum(t, h, k):
        total = part[t, h, x, k, upper].astype(jnp.float32)
        for e in range(nx - 1):
            total += xrecv[t, h, e, k].astype(jnp.float32)
        return total

    def z_wait(t, h, lo, n, sem):
        arrived = zrecv.at[t, h, pl.ds(lo, n)]
        remote(arrived, arrived, z_send.at[t, h], z_recv.at[t, h, sem], sibling).wait_recv()

    def x_run(t, h, first, past):
        for g in range(first, past):
            lo, hi = BOUNDS[g], BOUNDS[g + 1]
            arrived = xrecv.at[t, h, :, pl.ds(lo, hi - lo)]
            remote(arrived, arrived, x_send.at[t, h], x_recv.at[t, h, g], sibling).wait_recv()
            for k in range(lo, hi):
                total = x_sum(t, h, k)
                if k == OWN:
                    zown[t, h] = total
                    continue
                slot, sem = (k, (0, 0, 1, 2, 2)[k]) if k < OWN else (k - 1, 2)
                if k == 6:
                    z_wait(t, h, 0, 2, 0)
                    total += zrecv[t, h, 0].astype(jnp.float32) + zrecv[t, h, 1].astype(jnp.float32)
                if k == 7:
                    z_wait(t, h, 2, 1, 1)
                    total += zrecv[t, h, 2].astype(jnp.float32)
                zsend[t, h, slot] = total.astype(jnp.bfloat16)
                remote(zsend.at[t, h, slot], zrecv.at[t, h, slot], z_send.at[t, h], z_recv.at[t, h, sem],
                       at_z(STEPS[k] * turn)).start()

    def zf_block(t, h, k):
        return part.at[t, h, :, k, lower]

    def zf_send_to(t, h, source, slot, sem, d):
        remote(source, zfrecv.at[t, h, slot], zf_send.at[t, h], zf_recv.at[t, h, sem], at_z(d)).start()

    def zf_start(t, h):
        zf_send_to(t, h, zf_block(t, h, 0), 0, 0, 2 * turn)
        zf_send_to(t, h, zf_block(t, h, 1), 1, 0, turn)
        zf_send_to(t, h, zf_block(t, h, 2), 2, 1, -turn)
        zf_send_to(t, h, zf_block(t, h, 3), 3, 2, turn)
        zf_send_to(t, h, zf_block(t, h, 4), 4, 2, -turn)

    def zf_wait(t, h, lo, n, sem):
        arrived = zfrecv.at[t, h, pl.ds(lo, n)]
        remote(arrived, arrived, zf_send.at[t, h], zf_recv.at[t, h, sem], sibling).wait_recv()

    def zf_own(t, h, k):
        return part[t, h, :, k, lower].astype(jnp.float32)

    def zf_mid(t, h):
        zf_wait(t, h, 0, 2, 0)
        total = zf_own(t, h, 6) + zfrecv[t, h, 0].astype(jnp.float32) + zfrecv[t, h, 1].astype(jnp.float32)
        zfmid[t, h, 0] = total.astype(jnp.bfloat16)
        zf_send_to(t, h, zfmid.at[t, h, 0], 5, 2, 2 * turn)
        zf_wait(t, h, 2, 1, 1)
        total = zf_own(t, h, 7) + zfrecv[t, h, 2].astype(jnp.float32)
        zfmid[t, h, 1] = total.astype(jnp.bfloat16)
        zf_send_to(t, h, zfmid.at[t, h, 1], 6, 2, -2 * turn)

    def zf_end(t, h):
        zf_wait(t, h, 3, 4, 2)
        total = zf_own(t, h, OWN)
        for slot in range(3, 7):
            total += zfrecv[t, h, slot].astype(jnp.float32)
        xfsend[t, h] = total.astype(jnp.bfloat16)
        for e in (2, 1, 3):
            remote(xfsend.at[t, h, lax.rem(x + e, nx)], xfrecv.at[t, h, e - 1], xf_send.at[t, h], xf_recv.at[t, h], at_x(e)).start()

    def finish(t, h):
        z_wait(t, h, 3, 4, 2)
        total = zown[t, h]
        for slot in range(3, 7):
            total += zrecv[t, h, slot].astype(jnp.float32)
        lanes = slice(h * LANES, (h + 1) * LANES)

        def store(part_rows, total):
            current = 0.9 * total + 0.1 * logits[part_rows, lanes]
            if t + 1 < HOPS:
                panel[t + 1][h][row, part_rows] = current.astype(jnp.bfloat16)
            else:
                out[part_rows, lanes] = current

        store(slice(0, ROWS), total)
        arrived = xfrecv.at[t, h]
        remote(arrived, arrived, xf_send.at[t, h], xf_recv.at[t, h], sibling).wait_recv()
        total = xfsend[t, h, x].astype(jnp.float32)
        for e in range(nx - 1):
            total += xfrecv[t, h, e].astype(jnp.float32)
        store(slice(ROWS, tile), total)

    def sent(t, h):
        some = panel[t][h].at[pl.ds(0, ny - 1)]
        remote(some, some, ag_send.at[t, h], ag_recv.at[t, h, 0], sibling).wait_send()
        some = panel[t][h].at[pl.ds(0, ny)]
        remote(some, some, sib_send.at[t, h], sib_recv.at[t, h], sibling).wait_send()
        some = xrecv.at[t, h]
        remote(some, some, x_send.at[t, h], x_recv.at[t, h, 0], sibling).wait_send()
        some = zsend.at[t, h]
        remote(some, some, z_send.at[t, h], z_recv.at[t, h, 0], sibling).wait_send()
        some = zfrecv.at[t, h]
        remote(some, some, zf_send.at[t, h], zf_recv.at[t, h, 0], sibling).wait_send()
        some = xfrecv.at[t, h]
        remote(some, some, xf_send.at[t, h], xf_recv.at[t, h], sibling).wait_send()

    groups = len(BOUNDS) - 1

    def open_all(t, h):
        zf_start(t, h)
        for g in range(groups):
            x_start(t, h, g)

    gather_start(0, 0)

    prod[cap] = jnp.zeros((tile, LANES), jnp.bfloat16)
    count = counts_s[0, 0]

    def find(r, carry):
        place = jnp.int32(0)
        step = cap
        while step:
            tried = place + step
            fits = (tried <= count) & (rows_s[0, 0, jnp.minimum(tried, cap) - 1] <= r)
            place = jnp.where(fits, tried, place)
            step //= 2
        found = (place > 0) & (rows_s[0, 0, jnp.maximum(place - 1, 0)] == r)
        last[r] = jnp.where(found, place - 1, cap)
        return carry

    loads[1].wait()
    loads[2].wait()
    lax.fori_loop(0, ncol // 2, find, 0)
    gather_mid(0, 0)
    gather_start(0, 1)
    lax.fori_loop(ncol // 2, ncol, find, 0)
    loads[3].wait()

    gather_finish(0, 0)
    products(0, 0)
    open_all(0, 0)
    gather_mid(0, 1)
    x_run(0, 0, 0, 1)
    zf_mid(0, 0)
    gather_finish(0, 1)
    products(0, 1)
    open_all(0, 1)
    x_run(0, 0, 1, groups)
    zf_end(0, 0)
    x_run(0, 1, 0, 1)
    zf_mid(0, 1)
    finish(0, 0)
    gather_start(1, 0)
    x_run(0, 1, 1, groups)
    zf_end(0, 1)
    gather_mid(1, 0)
    finish(0, 1)
    gather_start(1, 1)
    gather_finish(1, 0)
    products(1, 0)
    open_all(1, 0)
    gather_mid(1, 1)
    x_run(1, 0, 0, 1)
    zf_mid(1, 0)
    gather_finish(1, 1)
    products(1, 1)
    open_all(1, 1)
    sent(0, 0)
    sent(0, 1)
    x_run(1, 0, 1, groups)
    zf_end(1, 0)
    x_run(1, 1, 0, 1)
    zf_mid(1, 1)
    finish(1, 0)
    x_run(1, 1, 1, groups)
    zf_end(1, 1)
    sent(1, 0)
    finish(1, 1)
    sent(1, 1)


def solution(mesh):
    nrow, ncol = mesh.shape["row"], mesh.shape["col"]
    ny = nrow // 2
    nx = 4 if ncol == 32 else 2
    nz = ncol // nx

    def body(logits, tile_values, tile_rows, tile_cols, tile_counts):
        cap, tile = tile_values.shape[2], tile_values.shape[3]
        half = jnp.bfloat16
        dma = pltpu.SemaphoreType.DMA
        both = (HOPS, HALVES)
        return pl.pallas_call(
            functools.partial(kernel, nx, ny, nz),
            out_shape=jax.ShapeDtypeStruct(logits.shape, jnp.float32),
            in_specs=[
                pl.BlockSpec(memory_space=pl.ANY),
                pl.BlockSpec(memory_space=pl.ANY),
                pl.BlockSpec(memory_space=pl.ANY),
                pl.BlockSpec(memory_space=pltpu.SMEM),
                pl.BlockSpec(memory_space=pl.ANY),
            ],
            out_specs=pl.BlockSpec(memory_space=pltpu.VMEM),
            scratch_shapes=[
                pltpu.VMEM((cap, tile, tile), half),
                pltpu.VMEM((cap + 1, tile, LANES), half),
                pltpu.SMEM((ncol,), jnp.int32),
                pltpu.SMEM((1, 1, cap), jnp.int32),
                pltpu.SMEM((1, 1, cap), jnp.int32),
                pltpu.VMEM(logits.shape, jnp.float32),
                *[pltpu.VMEM((nrow, tile, LANES), half) for unused in range(HOPS * HALVES)],
                pltpu.VMEM((*both, nx, nz, tile, LANES), half),
                pltpu.VMEM((*both, nx - 1, nz, ROWS, LANES), half),
                pltpu.VMEM((*both, nz - 1, ROWS, LANES), half),
                pltpu.VMEM((*both, nz - 1, ROWS, LANES), half),
                pltpu.VMEM((*both, ROWS, LANES), jnp.float32),
                pltpu.VMEM((*both, 7, nx, tile - ROWS, LANES), half),
                pltpu.VMEM((*both, 2, nx, tile - ROWS, LANES), half),
                pltpu.VMEM((*both, nx, tile - ROWS, LANES), half),
                pltpu.VMEM((*both, nx - 1, tile - ROWS, LANES), half),
                dma((4,)),
                dma(both),
                dma((*both, 7)),
                dma(both),
                dma(both),
                dma(both),
                dma((*both, nz)),
                dma(both),
                dma((*both, 3)),
                dma(both),
                dma((*both, 3)),
                dma(both),
                dma(both),
            ],
            compiler_params=pltpu.CompilerParams(
                collective_id=0, has_side_effects=True, vmem_limit_bytes=58 * 2**20
            ),
            name="propagate",
        )(tile_values, tile_rows, tile_cols, tile_counts, logits)

    return jax.shard_map(
        body,
        mesh=mesh,
        in_specs=(
            P(("row", "col"), None),
            P("row", "col", None, None, None),
            P("row", "col", None),
            P("row", "col", None),
            P("row", "col"),
        ),
        out_specs=P(("row", "col"), None),
        check_vma=False,
    )
```

```python
import functools

import jax
import jax.numpy as jnp
from jax import lax
from jax.experimental import pallas as pl
from jax.experimental.pallas import tpu as pltpu
from jax.sharding import PartitionSpec as P

HOPS = 2
HALVES = 2
LANES = 128
UNROLL = 128
ROWS = 80
BOUNDS = (0, 3, 6, 8)
OFFSETS = (4, 3, -3, 1, -1, 0, 2, -2)
STEPS = (2, 1, -1, 1, -1, 0, 2, -2)
OWN = 5
MESH = pl.DeviceIdType.MESH


def kernel(nx, ny, nz, *refs):
    (tiles_hbm, rows_hbm, cols_hbm, counts_s, logits_hbm, out, tv, prod, last, rows_s, cols_s, logits,
     panel00, panel01, panel10, panel11, part, xrecv, zsend, zrecv, zown, zfrecv, zfmid, xfsend, xfrecv,
     in_sems, ag_send, ag_recv, sib_send, sib_recv, x_send, x_recv, z_send, z_recv,
     zf_send, zf_recv, xf_send, xf_recv) = refs
    panel = ((panel00, panel01), (panel10, panel11))
    cap, tile = tv.shape[0], tv.shape[1]
    nrow, ncol = 2 * ny, nx * nz
    row, col = lax.axis_index("row"), lax.axis_index("col")
    x, z, core = col // nz, lax.rem(col, nz), lax.rem(row, 2)
    sibling = (row + 1 - 2 * core, col)
    turn = 1 - 2 * core
    upper, lower = pl.ds(0, ROWS), pl.ds(ROWS, tile - ROWS)

    def at_y(d):
        return (lax.rem(row + 2 * (d + ny), nrow), col)

    def at_x(d):
        return (row, lax.rem(col + nz * d, ncol))

    def at_z(d):
        return (row, x * nz + lax.rem(z + d + nz, nz))

    barrier = pltpu.get_barrier_semaphore()
    ways = (1, -1, 2, -2)
    peers = [at_y(d) for d in ways] + [at_x(d) for d in range(1, nx)] + [at_z(d) for d in ways] + [sibling]
    for peer in peers:
        pl.semaphore_signal(barrier, inc=1, device_id=peer, device_id_type=MESH)
    loads = [
        pltpu.make_async_copy(logits_hbm, logits, in_sems.at[0]),
        pltpu.make_async_copy(rows_hbm, rows_s, in_sems.at[1]),
        pltpu.make_async_copy(cols_hbm, cols_s, in_sems.at[2]),
        pltpu.make_async_copy(tiles_hbm.at[0, 0], tv, in_sems.at[3]),
    ]
    for load in loads:
        load.start()
    loads[0].wait()
    for h in range(HALVES):
        panel[0][h][row] = logits[:, h * LANES:(h + 1) * LANES].astype(jnp.bfloat16)
    pl.semaphore_wait(barrier, len(peers))

    def remote(src, dst, send_sem, recv_sem, device):
        return pltpu.make_async_remote_copy(src_ref=src, dst_ref=dst, send_sem=send_sem, recv_sem=recv_sem,
                                            device_id=device, device_id_type=MESH)

    def gather_send(t, h, block, slot, d):
        p = panel[t][h]
        remote(p.at[block], p.at[block], ag_send.at[t, h], ag_recv.at[t, h, slot], at_y(d)).start()

    def gather_start(t, h):
        p = panel[t][h]
        for slot, d in enumerate((2, -2, 1, -1)):
            gather_send(t, h, row, slot, d)
        remote(p.at[row], p.at[row], sib_send.at[t, h], sib_recv.at[t, h], sibling).start()

    def gather_wait(t, h, slot, d):
        p = panel[t][h]
        source = lax.rem(row + nrow - 2 * d, nrow)
        block = p.at[source]
        remote(block, block, ag_send.at[t, h], ag_recv.at[t, h, slot], sibling).wait_recv()
        remote(block, block, sib_send.at[t, h], sib_recv.at[t, h], sibling).start()
        return source

    def gather_mid(t, h):
        first = []
        for slot, d in enumerate((2, -2)):
            p = panel[t][h]
            source = lax.rem(row + nrow - 2 * d, nrow)
            block = p.at[source]
            remote(block, block, ag_send.at[t, h], ag_recv.at[t, h, slot], sibling).wait_recv()
            gather_send(t, h, source, 4 + slot, d // 2)
            first.append(source)
        gather_send(t, h, lax.rem(row + nrow - 4 * turn, nrow), 6, 2 * turn)
        for source in first:
            block = panel[t][h].at[source]
            remote(block, block, sib_send.at[t, h], sib_recv.at[t, h], sibling).start()

    def gather_finish(t, h):
        for slot, d in ((2, 1), (3, -1), (4, 3), (5, -3), (6, 4)):
            gather_wait(t, h, slot, d)
        most = panel[t][h].at[pl.ds(0, ny)]
        remote(most, most, sib_send.at[t, h], sib_recv.at[t, h], sibling).wait_recv()

    def products(t, h):
        p = panel[t][h]
        unroll = min(UNROLL, cap)

        def group(g, total):
            terms = [
                jnp.dot(tv[g * unroll + u], p[cols_s[0, 0, g * unroll + u]], preferred_element_type=jnp.float32)
                for u in range(unroll)
            ]
            for u in range(unroll):
                s = g * unroll + u
                same = (rows_s[0, 0, s] == rows_s[0, 0, jnp.maximum(s - 1, 0)]).astype(jnp.float32)
                total = total * same + terms[u]
                prod[s] = total.astype(jnp.bfloat16)
            return total

        lax.fori_loop(0, cap // unroll, group, jnp.zeros((tile, LANES), jnp.float32))

        for k, d in enumerate(OFFSETS):
            block = lax.rem(z + d * turn + nz, nz)
            for target in range(nx):
                part[t, h, target, k] = prod[last[target * nz + block]]

    def x_start(t, h, g):
        some = pl.ds(BOUNDS[g], BOUNDS[g + 1] - BOUNDS[g])
        for e in (2, 1, 3):
            target = lax.rem(x + e, nx)
            remote(part.at[t, h, target, some, upper], xrecv.at[t, h, e - 1, some], x_send.at[t, h], x_recv.at[t, h, g], at_x(e)).start()

    def x_sum(t, h, k):
        total = part[t, h, x, k, upper].astype(jnp.float32)
        for e in range(nx - 1):
            total += xrecv[t, h, e, k].astype(jnp.float32)
        return total

    def z_wait(t, h, lo, n, sem):
        arrived = zrecv.at[t, h, pl.ds(lo, n)]
        remote(arrived, arrived, z_send.at[t, h], z_recv.at[t, h, sem], sibling).wait_recv()

    def x_run(t, h, first, past):
        for g in range(first, past):
            lo, hi = BOUNDS[g], BOUNDS[g + 1]
            arrived = xrecv.at[t, h, :, pl.ds(lo, hi - lo)]
            remote(arrived, arrived, x_send.at[t, h], x_recv.at[t, h, g], sibling).wait_recv()
            for k in range(lo, hi):
                total = x_sum(t, h, k)
                if k == OWN:
                    zown[t, h] = total
                    continue
                slot, sem = (k, (0, 0, 1, 2, 2)[k]) if k < OWN else (k - 1, 2)
                if k == 6:
                    z_wait(t, h, 0, 2, 0)
                    total += zrecv[t, h, 0].astype(jnp.float32) + zrecv[t, h, 1].astype(jnp.float32)
                if k == 7:
                    z_wait(t, h, 2, 1, 1)
                    total += zrecv[t, h, 2].astype(jnp.float32)
                zsend[t, h, slot] = total.astype(jnp.bfloat16)
                remote(zsend.at[t, h, slot], zrecv.at[t, h, slot], z_send.at[t, h], z_recv.at[t, h, sem],
                       at_z(STEPS[k] * turn)).start()

    def zf_block(t, h, k):
        return part.at[t, h, :, k, lower]

    def zf_send_to(t, h, source, slot, sem, d):
        remote(source, zfrecv.at[t, h, slot], zf_send.at[t, h], zf_recv.at[t, h, sem], at_z(d)).start()

    def zf_start(t, h):
        zf_send_to(t, h, zf_block(t, h, 0), 0, 0, 2 * turn)
        zf_send_to(t, h, zf_block(t, h, 1), 1, 0, turn)
        zf_send_to(t, h, zf_block(t, h, 2), 2, 1, -turn)
        zf_send_to(t, h, zf_block(t, h, 3), 3, 2, turn)
        zf_send_to(t, h, zf_block(t, h, 4), 4, 2, -turn)

    def zf_wait(t, h, lo, n, sem):
        arrived = zfrecv.at[t, h, pl.ds(lo, n)]
        remote(arrived, arrived, zf_send.at[t, h], zf_recv.at[t, h, sem], sibling).wait_recv()

    def zf_own(t, h, k):
        return part[t, h, :, k, lower].astype(jnp.float32)

    def zf_mid(t, h):
        zf_wait(t, h, 0, 2, 0)
        total = zf_own(t, h, 6) + zfrecv[t, h, 0].astype(jnp.float32) + zfrecv[t, h, 1].astype(jnp.float32)
        zfmid[t, h, 0] = total.astype(jnp.bfloat16)
        zf_send_to(t, h, zfmid.at[t, h, 0], 5, 2, 2 * turn)
        zf_wait(t, h, 2, 1, 1)
        total = zf_own(t, h, 7) + zfrecv[t, h, 2].astype(jnp.float32)
        zfmid[t, h, 1] = total.astype(jnp.bfloat16)
        zf_send_to(t, h, zfmid.at[t, h, 1], 6, 2, -2 * turn)

    def zf_end(t, h):
        zf_wait(t, h, 3, 4, 2)
        total = zf_own(t, h, OWN)
        for slot in range(3, 7):
            total += zfrecv[t, h, slot].astype(jnp.float32)
        xfsend[t, h] = total.astype(jnp.bfloat16)
        for e in (2, 1, 3):
            remote(xfsend.at[t, h, lax.rem(x + e, nx)], xfrecv.at[t, h, e - 1], xf_send.at[t, h], xf_recv.at[t, h], at_x(e)).start()

    def finish(t, h):
        z_wait(t, h, 3, 4, 2)
        total = zown[t, h]
        for slot in range(3, 7):
            total += zrecv[t, h, slot].astype(jnp.float32)
        lanes = slice(h * LANES, (h + 1) * LANES)

        def store(part_rows, total):
            current = 0.9 * total + 0.1 * logits[part_rows, lanes]
            if t + 1 < HOPS:
                panel[t + 1][h][row, part_rows] = current.astype(jnp.bfloat16)
            else:
                out[part_rows, lanes] = current

        store(slice(0, ROWS), total)
        arrived = xfrecv.at[t, h]
        remote(arrived, arrived, xf_send.at[t, h], xf_recv.at[t, h], sibling).wait_recv()
        total = xfsend[t, h, x].astype(jnp.float32)
        for e in range(nx - 1):
            total += xfrecv[t, h, e].astype(jnp.float32)
        store(slice(ROWS, tile), total)

    def sent(t, h):
        some = panel[t][h].at[pl.ds(0, ny - 1)]
        remote(some, some, ag_send.at[t, h], ag_recv.at[t, h, 0], sibling).wait_send()
        some = panel[t][h].at[pl.ds(0, ny)]
        remote(some, some, sib_send.at[t, h], sib_recv.at[t, h], sibling).wait_send()
        some = xrecv.at[t, h]
        remote(some, some, x_send.at[t, h], x_recv.at[t, h, 0], sibling).wait_send()
        some = zsend.at[t, h]
        remote(some, some, z_send.at[t, h], z_recv.at[t, h, 0], sibling).wait_send()
        some = zfrecv.at[t, h]
        remote(some, some, zf_send.at[t, h], zf_recv.at[t, h, 0], sibling).wait_send()
        some = xfrecv.at[t, h]
        remote(some, some, xf_send.at[t, h], xf_recv.at[t, h], sibling).wait_send()

    groups = len(BOUNDS) - 1

    def open_all(t, h):
        zf_start(t, h)
        for g in range(groups):
            x_start(t, h, g)

    gather_start(0, 0)

    prod[cap] = jnp.zeros((tile, LANES), jnp.bfloat16)
    count = counts_s[0, 0]

    def find(r, carry):
        place = jnp.int32(0)
        step = cap
        while step:
            tried = place + step
            fits = (tried <= count) & (rows_s[0, 0, jnp.minimum(tried, cap) - 1] <= r)
            place = jnp.where(fits, tried, place)
            step //= 2
        found = (place > 0) & (rows_s[0, 0, jnp.maximum(place - 1, 0)] == r)
        last[r] = jnp.where(found, place - 1, cap)
        return carry

    loads[1].wait()
    loads[2].wait()
    lax.fori_loop(0, ncol // 2, find, 0)
    gather_mid(0, 0)
    gather_start(0, 1)
    lax.fori_loop(ncol // 2, ncol, find, 0)
    loads[3].wait()

    gather_finish(0, 0)
    products(0, 0)
    open_all(0, 0)
    gather_mid(0, 1)
    gather_finish(0, 1)
    products(0, 1)
    x_run(0, 0, 0, 1)
    zf_mid(0, 0)
    open_all(0, 1)
    x_run(0, 0, 1, groups)
    zf_end(0, 0)
    x_run(0, 1, 0, 1)
    zf_mid(0, 1)
    finish(0, 0)
    gather_start(1, 0)
    x_run(0, 1, 1, groups)
    zf_end(0, 1)
    gather_mid(1, 0)
    finish(0, 1)
    gather_start(1, 1)
    gather_finish(1, 0)
    products(1, 0)
    open_all(1, 0)
    gather_mid(1, 1)
    x_run(1, 0, 0, 1)
    zf_mid(1, 0)
    gather_finish(1, 1)
    products(1, 1)
    open_all(1, 1)
    sent(0, 0)
    sent(0, 1)
    x_run(1, 0, 1, groups)
    zf_end(1, 0)
    x_run(1, 1, 0, 1)
    zf_mid(1, 1)
    x_run(1, 1, 1, groups)
    zf_end(1, 1)
    finish(1, 0)
    sent(1, 0)
    finish(1, 1)
    sent(1, 1)


def solution(mesh):
    nrow, ncol = mesh.shape["row"], mesh.shape["col"]
    ny = nrow // 2
    nx = 4 if ncol == 32 else 2
    nz = ncol // nx

    def body(logits, tile_values, tile_rows, tile_cols, tile_counts):
        cap, tile = tile_values.shape[2], tile_values.shape[3]
        half = jnp.bfloat16
        dma = pltpu.SemaphoreType.DMA
        both = (HOPS, HALVES)
        return pl.pallas_call(
            functools.partial(kernel, nx, ny, nz),
            out_shape=jax.ShapeDtypeStruct(logits.shape, jnp.float32),
            in_specs=[
                pl.BlockSpec(memory_space=pl.ANY),
                pl.BlockSpec(memory_space=pl.ANY),
                pl.BlockSpec(memory_space=pl.ANY),
                pl.BlockSpec(memory_space=pltpu.SMEM),
                pl.BlockSpec(memory_space=pl.ANY),
            ],
            out_specs=pl.BlockSpec(memory_space=pltpu.VMEM),
            scratch_shapes=[
                pltpu.VMEM((cap, tile, tile), half),
                pltpu.VMEM((cap + 1, tile, LANES), half),
                pltpu.SMEM((ncol,), jnp.int32),
                pltpu.SMEM((1, 1, cap), jnp.int32),
                pltpu.SMEM((1, 1, cap), jnp.int32),
                pltpu.VMEM(logits.shape, jnp.float32),
                *[pltpu.VMEM((nrow, tile, LANES), half) for unused in range(HOPS * HALVES)],
                pltpu.VMEM((*both, nx, nz, tile, LANES), half),
                pltpu.VMEM((*both, nx - 1, nz, ROWS, LANES), half),
                pltpu.VMEM((*both, nz - 1, ROWS, LANES), half),
                pltpu.VMEM((*both, nz - 1, ROWS, LANES), half),
                pltpu.VMEM((*both, ROWS, LANES), jnp.float32),
                pltpu.VMEM((*both, 7, nx, tile - ROWS, LANES), half),
                pltpu.VMEM((*both, 2, nx, tile - ROWS, LANES), half),
                pltpu.VMEM((*both, nx, tile - ROWS, LANES), half),
                pltpu.VMEM((*both, nx - 1, tile - ROWS, LANES), half),
                dma((4,)),
                dma(both),
                dma((*both, 7)),
                dma(both),
                dma(both),
                dma(both),
                dma((*both, nz)),
                dma(both),
                dma((*both, 3)),
                dma(both),
                dma((*both, 3)),
                dma(both),
                dma(both),
            ],
            compiler_params=pltpu.CompilerParams(
                collective_id=0, has_side_effects=True, vmem_limit_bytes=58 * 2**20
            ),
            name="propagate",
        )(tile_values, tile_rows, tile_cols, tile_counts, logits)

    return jax.shard_map(
        body,
        mesh=mesh,
        in_specs=(
            P(("row", "col"), None),
            P("row", "col", None, None, None),
            P("row", "col", None),
            P("row", "col", None),
            P("row", "col"),
        ),
        out_specs=P(("row", "col"), None),
        check_vma=False,
    )
```
